256 devices in a mesh: dp: 16 (over x, z_hi), tensor: 16 (over y, z_lo, core).
Axes of the slice: x: 4, y: 4, z: 8 (z_hi: 4, z_lo: 2; z = z_hi * 2 + z_lo), core: 2. Of those that a mesh axis runs over, the one named last changes fastest.
Arguments:
- hidden_in: bfloat16 [128, 16384], P('dp'), may hold values from -6 to 6
- norm_gain: float32 [16384], replicated, may hold values from 0.1 to 1.9
- w_query: bfloat16 [16384, 16384], P('dp', 'tensor'), may hold values from -0.046875 to 0.046875
- w_keyval: bfloat16 [16384, 2048], P('dp', 'tensor'), may hold values from -0.046875 to 0.046875
- w_out: bfloat16 [16384, 16384], P('tensor', 'dp'), may hold values from -0.046875 to 0.046875
- key_cache: bfloat16 [128, 16, 2048, 128], P('dp', 'tensor'), may hold values from -320 to 320
- value_cache: bfloat16 [128, 16, 2048, 128], P('dp', 'tensor'), may hold values from -6 to 6
- parent: int32 [128], P('dp'), may hold values from 0 to 127, as said below
- lengths: int32 [128], P('dp'), may hold values from 1 to 4096, as said below
Outputs:
- attended: bfloat16 [128, 16384], P('dp')
The draws below stay inside these ranges and needn't reach their ends.
Inputs may be any that keep to these rules, and one draw needn't show every extreme that they name: parent[r] // 8 == r // 8: a row continues a cache of its own index of dp. `lengths`: every row has at least one cached position, and some row has all 4096.
All inputs are finite; a program needn't handle non-finite values.
Results may differ from the reference program's by a relative error of at most 0.012.
The reference program's roundings to bfloat16 on the way (of `normed`, `queries` and `heads`) count: a program that leaves them out, or rounds other values in their place, can miss the bound.
Values may be sent and summed in bfloat16 or wider, within the bound.
No kernel may reach another device: no remote copies, remote signals or barrier semaphores. Data moves between devices by JAX's collectives and lax.ppermute only.
A program may use at most 64 MiB of HBM per device.

```python
import jax
import jax.numpy as jnp
from jax import lax

D = 16384
HD = 128
ROWS_DEV = 8
CTX = 4096
HALF = 2048
ROWS = 128
HQ = 128
KVH = 8
SHARDS = 16
GROUP = 16


def draw_key_cache(key, part):
    key = jax.random.fold_in(key, 11)
    base_key = jax.random.fold_in(key, 0)
    shape = (ROWS, SHARDS, HALF, HD)
    values = jnp.clip(jax.random.normal(base_key, shape, jnp.float32) * 2.0, -12.0, 12.0)
    return values.astype(jnp.bfloat16)


def draw_parent(key, part):
    key = jax.random.fold_in(key, 23)
    offsets = jax.random.randint(key, (ROWS,), 0, ROWS_DEV, dtype=jnp.int32)
    rowids = jnp.arange(ROWS, dtype=jnp.int32)
    chosen = rowids // ROWS_DEV * ROWS_DEV + offsets
    chosen = jnp.where(rowids == 0, 0, chosen)
    return jnp.where(rowids == ROWS - 1, ROWS - 1, chosen).astype(jnp.int32)


def draw_lengths(key, part):
    key = jax.random.fold_in(key, 37)
    raw_key, factor_key, pick_key = jax.random.split(key, 3)
    raw = jax.random.randint(raw_key, (ROWS,), 0, CTX, dtype=jnp.int32)
    factor = jax.random.randint(factor_key, (ROWS // ROWS_DEV,), 1, 5, dtype=jnp.int32)
    factor_rows = jnp.repeat(factor, ROWS_DEV)
    drawn = 1 + raw * factor_rows // 4
    pick = jax.random.randint(pick_key, (), 0, ROWS, dtype=jnp.int32)
    rowids = jnp.arange(ROWS, dtype=jnp.int32)
    return jnp.where(rowids == pick, CTX, drawn).astype(jnp.int32)


def shard_levels(own_key, dims, shards, least, largest):
    gain, own = 1.0, jax.random.fold_in(own_key, 6)
    for position, shards_of in shards:
        draws = jnp.exp(jax.random.uniform(jax.random.fold_in(own, position), (shards_of,), jnp.float32, least / len(shards), largest / len(shards)))
        gain = gain * jnp.repeat(draws, dims[position] // shards_of).reshape([-1 if axis == position else 1 for axis in range(len(dims))])
    return gain


def scatter_about(own_key, extent, width, bound, cuts=(), kind=jnp.bfloat16):
    gain = shard_levels(own_key, extent, cuts, -0.22, 0.18) if cuts else 1.0
    values = jax.random.normal(own_key, extent, jnp.float32) * width * gain
    return jnp.minimum(jnp.maximum(values, -bound), bound).astype(kind)


def setup_inputs(seed: int = 0) -> dict:
    arg_keys = jax.random.split(jax.random.key(seed), 10)
    hidden_in = scatter_about(arg_keys[0], (ROWS, D), 1.0, 6.0, ((0, 16),))
    norm_gain = jnp.clip(1.0 + 0.18 * jax.random.normal(arg_keys[1], (D,), jnp.float32), 0.1, 1.9)
    w_query = scatter_about(arg_keys[2], (D, HQ * HD), D ** -0.5, 0.046875, ((0, 16), (1, 16)))
    w_keyval = scatter_about(arg_keys[3], (D, SHARDS * HD), D ** -0.5, 0.046875, ((0, 16), (1, 16)))
    w_out = scatter_about(arg_keys[4], (HQ * HD, D), (HQ * HD) ** -0.5, 0.046875, ((0, 16), (1, 16)))
    key_cache = draw_key_cache(jax.random.fold_in(arg_keys[9], 71), 0)
    value_cache = scatter_about(arg_keys[6], (ROWS, SHARDS, HALF, HD), 1.0, 6.0, ((0, 16), (1, 16)))
    parent = draw_parent(jax.random.fold_in(arg_keys[9], 71), 0)
    lengths = draw_lengths(jax.random.fold_in(arg_keys[9], 71), 0)
    return dict(hidden_in=hidden_in, norm_gain=norm_gain, w_query=w_query, w_keyval=w_keyval, w_out=w_out, key_cache=key_cache, value_cache=value_cache, parent=parent, lengths=lengths)


def rotate(t, pos):
    half = t.shape[-1] // 2
    inv = jnp.power(jnp.float32(500000.0), -jnp.arange(half, dtype=jnp.float32) * 2.0 / t.shape[-1])
    angle = pos[..., None] * inv
    cosine = jnp.cos(angle)
    sine = jnp.sin(angle)
    first = t[..., :half]
    second = t[..., half:]
    return jnp.concatenate([first * cosine - second * sine, second * cosine + first * sine], axis=-1)

def reference(hidden_in, norm_gain, w_query, w_keyval, w_out, key_cache, value_cache, parent, lengths):
    xf = hidden_in.astype(jnp.float32)
    meansq = lax.optimization_barrier(jnp.mean(xf * xf, axis=-1, keepdims=True))
    normed = (xf * lax.rsqrt(meansq + 1e-05) * norm_gain).astype(jnp.bfloat16)
    qraw = jnp.dot(normed, w_query, preferred_element_type=jnp.float32)
    kvraw = jnp.dot(normed, w_keyval, preferred_element_type=jnp.float32).reshape(ROWS, KVH, 2, HD)
    pos = lengths.astype(jnp.float32)
    queries = rotate(qraw.reshape(ROWS, HQ, HD), pos[:, None]).astype(jnp.bfloat16)
    new_key = rotate(kvraw[:, :, 0], pos[:, None]).astype(jnp.bfloat16)
    new_value = kvraw[:, :, 1].astype(jnp.bfloat16)
    scale = HD ** (-0.5)

    def one_row(r):
        src = parent[r]
        keys = lax.dynamic_index_in_dim(key_cache, src, 0, keepdims=False).reshape(KVH, CTX, HD).astype(jnp.float32)
        values = lax.dynamic_index_in_dim(value_cache, src, 0, keepdims=False).reshape(KVH, CTX, HD).astype(jnp.float32)
        qrow = queries[r].reshape(KVH, GROUP, HD).astype(jnp.float32)
        scores = jnp.einsum('hgd,hcd->hgc', qrow, keys) * scale
        valid = jnp.arange(CTX, dtype=jnp.int32) < lengths[r]
        scores = jnp.where(valid[None, None, :], scores, -jnp.inf)
        newscore = jnp.einsum('hgd,hd->hg', qrow, new_key[r].astype(jnp.float32)) * scale
        top = jnp.maximum(lax.optimization_barrier(jnp.max(scores, axis=-1)), newscore)
        weights = jnp.exp(scores - top[..., None])
        newweight = jnp.exp(newscore - top)
        total = lax.optimization_barrier(jnp.sum(weights, axis=-1)) + newweight
        acc = jnp.einsum('hgc,hcd->hgd', weights.astype(jnp.bfloat16).astype(jnp.float32), values)
        acc = acc + newweight.astype(jnp.bfloat16).astype(jnp.float32)[..., None] * new_value[r].astype(jnp.float32)[:, None, :]
        return (acc / total[..., None]).reshape(HQ * HD).astype(jnp.bfloat16)
    heads = lax.map(one_row, jnp.arange(ROWS, dtype=jnp.int32))
    return jnp.dot(heads, w_out, preferred_element_type=jnp.float32).astype(jnp.bfloat16)
```

```python
import jax
import jax.numpy as jnp
from jax import lax
from jax.sharding import PartitionSpec as P


def row_groups(columns):
    return [[j * columns + (j ^ p) for p in range(columns)] for j in range(columns)]


def exchange(value, groups):
    return lax.all_to_all(
        value, ("dp", "tensor"), 0, 0, tiled=True, axis_index_groups=groups
    )


def swapped(value, axis, bit):
    mask = 2**bit
    pairs = [(source, source ^ mask) for source in range(lax.axis_size(axis))]
    return lax.ppermute(value, axis, pairs)


def rotate(t, pos):
    half = t.shape[-1] // 2
    inv = jnp.power(jnp.float32(500000.0), -jnp.arange(half, dtype=jnp.float32) * 2.0 / t.shape[-1])
    angle = pos[..., None] * inv
    cosine = jnp.cos(angle)
    sine = jnp.sin(angle)
    first = t[..., :half]
    second = t[..., half:]
    return jnp.concatenate(
        [first * cosine - second * sine, second * cosine + first * sine], axis=-1
    )


def per_device(
    hidden_in, norm_gain, w_query, w_keyval, w_out, key_cache, value_cache, parent, lengths
):
    rows_dev = hidden_in.shape[0]
    head_dim = key_cache.shape[3]
    half = key_cache.shape[2]
    cols_q = w_query.shape[1]
    heads_dev = cols_q // head_dim
    scale = head_dim ** (-0.5)
    xf = hidden_in.astype(jnp.float32)
    meansq = jnp.mean(xf * xf, axis=-1, keepdims=True)
    normed = (xf * lax.rsqrt(meansq + 1e-05) * norm_gain).astype(jnp.bfloat16)
    spread = lax.all_to_all(normed, "dp", split_axis=1, concat_axis=0, tiled=True)
    first = jnp.dot(spread, w_query, preferred_element_type=jnp.float32)
    second = jnp.dot(spread, w_keyval, preferred_element_type=jnp.float32)
    parts = lax.all_to_all(
        jnp.concatenate([first, second], axis=1).reshape(
            lax.axis_size("dp"), rows_dev, cols_q + second.shape[1]
        ),
        "dp",
        0,
        0,
        tiled=True,
    )
    projected = jnp.sum(parts, axis=0)
    pos = lengths.astype(jnp.float32)
    parity = lax.axis_index("tensor") % 2
    is_key = parity == 0
    queries_own = rotate(
        projected[:, :cols_q].reshape(rows_dev, heads_dev, head_dim), pos[:, None]
    ).astype(jnp.bfloat16)
    own_raw = projected[:, cols_q:]
    own_kv = jnp.where(is_key, rotate(own_raw, pos), own_raw).astype(jnp.bfloat16)
    queries_other, kv_other = swapped((queries_own, own_kv), "tensor", 0)
    queries = jnp.where(
        is_key,
        jnp.concatenate([queries_own, queries_other], axis=1),
        jnp.concatenate([queries_other, queries_own], axis=1),
    )
    new_key = jnp.where(is_key, own_kv, kv_other)
    new_value = jnp.where(is_key, kv_other, own_kv)
    local = parent - lax.axis_index("dp") * rows_dev
    keys = jnp.take(key_cache[:, 0], local, axis=0)
    values = jnp.take(value_cache[:, 0], local, axis=0)
    start_pos = parity * half
    position = start_pos + jnp.arange(half, dtype=jnp.int32)
    valid = position[None, :] < lengths[:, None]
    scores = jnp.einsum("rgd,rcd->rgc", queries, keys, preferred_element_type=jnp.float32) * scale
    scores = jnp.where(valid[:, None, :], scores, -jnp.inf)
    running = jnp.max(scores, axis=-1)
    safe = jnp.where(running == -jnp.inf, 0.0, running)
    weights = jnp.exp(scores - safe[..., None])
    summed = jnp.sum(weights, axis=-1)
    acc = jnp.einsum(
        "rgc,rcd->rgd", weights.astype(jnp.bfloat16), values, preferred_element_type=jnp.float32
    )
    newscore = (
        jnp.einsum("rgd,rd->rg", queries, new_key, preferred_element_type=jnp.float32) * scale
    )
    newscore = jnp.where(is_key, -jnp.inf, newscore)
    top = jnp.maximum(running, newscore)
    shrink = jnp.exp(running - top)
    newweight = jnp.exp(newscore - top)
    summed = summed * shrink + newweight
    acc = (
        acc * shrink[..., None]
        + newweight.astype(jnp.bfloat16).astype(jnp.float32)[..., None]
        * new_value.astype(jnp.float32)[:, None, :]
    )
    keep_acc = jnp.where(is_key, acc[:, :heads_dev], acc[:, heads_dev:])
    send_acc = jnp.where(is_key, acc[:, heads_dev:], acc[:, :heads_dev])
    keep_max = jnp.where(is_key, top[:, :heads_dev], top[:, heads_dev:])
    send_max = jnp.where(is_key, top[:, heads_dev:], top[:, :heads_dev])
    keep_sum = jnp.where(is_key, summed[:, :heads_dev], summed[:, heads_dev:])
    send_sum = jnp.where(is_key, summed[:, heads_dev:], summed[:, :heads_dev])
    other_acc, other_max, other_sum = swapped((send_acc, send_max, send_sum), "tensor", 0)
    highest = jnp.maximum(keep_max, other_max)
    mine_factor = jnp.exp(keep_max - highest)
    other_factor = jnp.exp(other_max - highest)
    total = keep_sum * mine_factor + other_sum * other_factor
    merged = (keep_acc * mine_factor[..., None] + other_acc * other_factor[..., None]) / total[
        ..., None
    ]
    heads = merged.reshape(rows_dev, heads_dev * head_dim).astype(jnp.bfloat16)
    blocks = lax.axis_size("dp")
    spread_heads = lax.all_to_all(
        lax.optimization_barrier(jnp.broadcast_to(heads[None], (blocks,) + heads.shape)),
        "dp",
        0,
        0,
        tiled=True,
    )
    partial_value = jnp.dot(
        spread_heads.reshape(blocks * rows_dev, heads.shape[1]),
        w_out,
        preferred_element_type=jnp.float32,
    ).astype(jnp.bfloat16)
    groups = row_groups(blocks)
    gathered = exchange(partial_value.reshape(blocks, rows_dev, w_out.shape[1]), groups)
    block = jnp.sum(gathered.astype(jnp.float32), axis=0).astype(jnp.bfloat16)
    pairs = [
        (j * blocks + t, (j ^ t) * blocks + t) for j in range(blocks) for t in range(blocks)
    ]
    block = lax.ppermute(block, ("dp", "tensor"), pairs)
    whole = exchange(
        lax.optimization_barrier(jnp.broadcast_to(block[None], (blocks,) + block.shape)), groups
    )
    result = jnp.transpose(whole, (1, 0, 2)).reshape(rows_dev, blocks * block.shape[1])
    return result


def solution(mesh):
    return jax.shard_map(
        per_device,
        mesh=mesh,
        in_specs=(
            P("dp", None),
            P(),
            P("dp", "tensor"),
            P("dp", "tensor"),
            P("tensor", "dp"),
            P("dp", "tensor", None, None),
            P("dp", "tensor", None, None),
            P("dp"),
            P("dp"),
        ),
        out_specs=P("dp", None),
        check_vma=False,
    )
```

```python
import jax
import jax.numpy as jnp
import numpy as np
from jax import lax
from jax.experimental import pallas as pl
from jax.experimental.pallas import tpu as pltpu
from jax.sharding import PartitionSpec as P

EPS = 1e-05
SCALE = 128.0
INVERSE = (500000.0 ** (-np.arange(64) * 2.0 / 128)).astype(np.float32)
VMEM = pl.BlockSpec(memory_space=pltpu.VMEM)
SMEM = pl.BlockSpec(memory_space=pltpu.SMEM)
HBM = pl.BlockSpec(memory_space=pltpu.HBM)


def index(x, z_hi, y, z_lo, core):
    return (x * 4 + z_hi) * 16 + y * 4 + z_lo * 2 + core


NEAR_GROUPS = [
    [index(x, z_hi, y, z_lo ^ (z_hi >> 1), core) for x in range(4) for z_hi in range(4)]
    for y in range(4)
    for z_lo in range(2)
    for core in range(2)
]


def holder(j, t):
    return t ^ 2 if t % 4 in (0, 2) else t


SUM_GROUPS = [[j * 16 + (j ^ p) for p in range(16)] for j in range(16)]
MOVES = [
    (j * 16 + t, (j ^ t) * 16 + holder(j, t)) for j in range(16) for t in range(16)
]
WHOLE_GROUPS = [[i * 16 + holder(p, i ^ p) for p in range(16)] for i in range(16)]


def exchange(value, groups):
    return lax.all_to_all(
        value, ("dp", "tensor"), 0, 0, tiled=True, axis_index_groups=groups
    )


def in_hbm(value):
    return pltpu.with_memory_space_constraint(value, pltpu.HBM)


def core_swap(value):
    return lax.ppermute(value, "tensor", [(t, t ^ 1) for t in range(16)])


def norm_kernel(
    hidden_hbm, gain_hbm, weight_hbm, lengths_hbm,
    out, weight, cosine_out, sine_out, kv_cosine_out, kv_sine_out,
    hidden, gain, lengths, sems,
):
    copies = [
        pltpu.make_async_copy(lengths_hbm, lengths, sems.at[0]),
        pltpu.make_async_copy(hidden_hbm, hidden, sems.at[1]),
        pltpu.make_async_copy(gain_hbm, gain, sems.at[2]),
        pltpu.make_async_copy(weight_hbm, weight, sems.at[3]),
    ]
    for copy in copies:
        copy.start()
    rows, hd = cosine_out.shape
    column = lax.broadcasted_iota(jnp.int32, (rows, hd), 1)
    row = lax.broadcasted_iota(jnp.int32, (rows, hd), 0)
    inv = jnp.zeros((rows, hd), jnp.float32)
    for k in range(hd // 2):
        inv = jnp.where(column % (hd // 2) == k, float(INVERSE[k]), inv)
    copies[0].wait()
    position = jnp.zeros((rows, hd), jnp.float32)
    for r in range(rows):
        position = jnp.where(row == r, lengths[r].astype(jnp.float32), position)
    angle = position * inv
    cosine = jnp.cos(angle)
    sine = jnp.where(column < hd // 2, -jnp.sin(angle), jnp.sin(angle))
    is_key = lax.axis_index("tensor") % 2 == 0
    cosine_out[...] = cosine
    sine_out[...] = sine
    kv_cosine_out[...] = jnp.where(is_key, cosine, 1.0)
    kv_sine_out[...] = jnp.where(is_key, sine, 0.0)
    copies[1].wait()
    xf = hidden[...].astype(jnp.float32)
    meansq = jnp.mean(xf * xf, axis=-1, keepdims=True)
    factor = lax.rsqrt(meansq + EPS)
    copies[2].wait()
    blocks, _, width = out.shape
    for k in range(blocks):
        part = slice(k * width, (k + 1) * width)
        out[k] = (xf[:, part] * factor * gain[:, part]).astype(jnp.bfloat16)
    copies[3].wait()


def rotate_kernel(total, cosine, sine, kv_cosine, kv_sine, out, turned):
    heads = total.shape[1] // 128 - 1
    for h in range(heads + 1):
        t = total[:, h * 128 : (h + 1) * 128]
        swapped = pltpu.roll(t, 64, 1)
        if h < heads:
            turned[:, h, :] = t * cosine[...] + swapped * sine[...]
        else:
            turned[:, h, :] = t * kv_cosine[...] + swapped * kv_sine[...]
    for r in range(8):
        out[r] = turned[r].astype(jnp.bfloat16)


def attention_kernel(
    parent, lengths, own, other, keys, value_cache, keep, send, values, weights, sems
):
    rows, _, half, hd = keys.shape
    base = lax.axis_index("dp") * rows
    parity = lax.axis_index("tensor") % 2
    copies = []
    for r in range(rows):
        src = parent[r] - base
        copies.append(
            pltpu.make_async_copy(value_cache.at[src, 0], values.at[r], sems.at[r])
        )
        copies[r].start()
    scale = hd ** (-0.5)
    second = parity == 1
    column = lax.broadcasted_iota(jnp.int32, (16, half), 1)
    found = []
    for r in range(rows):
        mine = own[r].astype(jnp.float32)
        theirs = other[r].astype(jnp.float32)
        queries = jnp.concatenate([mine[:8], theirs[:8]], axis=0)
        new_key = jnp.where(second, theirs[8:9], mine[8:9])
        new_value = jnp.where(second, mine[8:9], theirs[8:9])
        newscore = jnp.sum(queries * new_key, axis=-1, keepdims=True) * scale
        newscore = jnp.where(second, newscore, -jnp.inf)
        scores = lax.dot_general(
            queries.astype(jnp.bfloat16),
            keys[parent[r] - base, 0],
            (((1,), (1,)), ((), ())),
            preferred_element_type=jnp.float32,
        )
        limit = lengths[r] - parity * half
        scores = jnp.where(column < limit, scores * scale, -jnp.inf)
        top = jnp.maximum(jnp.max(scores, axis=-1, keepdims=True), newscore)
        weight = jnp.exp(scores - top)
        newweight = jnp.exp(newscore - top)
        total = jnp.sum(weight, axis=-1, keepdims=True) + newweight
        weights[r] = weight.astype(jnp.bfloat16)
        added = newweight.astype(jnp.bfloat16).astype(jnp.float32) * new_value
        found.append((added, top, total))
    for copy in copies:
        copy.wait()
    for r in range(rows):
        added, top, total = found[r]
        acc = jnp.dot(weights[r], values[r], preferred_element_type=jnp.float32) + added
        top = jnp.broadcast_to(top, acc.shape)
        total = jnp.broadcast_to(total, acc.shape)
        for k, part in enumerate((acc, top, total)):
            keep[:, r, k * hd : (k + 1) * hd] = part[:8]
            send[:, r, k * hd : (k + 1) * hd] = part[8:]


def merge_kernel(mine, theirs, out):
    hd = mine.shape[2] // 3
    for h in range(mine.shape[0]):
        a, b = mine[h], theirs[h]
        highest = jnp.maximum(a[:, hd : 2 * hd], b[:, hd : 2 * hd])
        fa = jnp.exp(a[:, hd : 2 * hd] - highest)
        fb = jnp.exp(b[:, hd : 2 * hd] - highest)
        total = a[:, 2 * hd :] * fa + b[:, 2 * hd :] * fb
        head = ((a[:, :hd] * fa + b[:, :hd] * fb) / total).astype(jnp.bfloat16)
        for k in range(out.shape[0]):
            out[k, :, h * hd : (h + 1) * hd] = head


def per_device(
    hidden_in, norm_gain, w_query, w_keyval, w_out, key_cache, value_cache, parent, lengths
):
    rows, d_model = hidden_in.shape
    hd = key_cache.shape[3]
    half = key_cache.shape[2]
    cols = w_query.shape[1]
    blocks = d_model // cols
    heads = cols // hd
    table = jax.ShapeDtypeStruct((rows, hd), jnp.float32)
    normed, w_keyval, *tables = pl.pallas_call(
        norm_kernel,
        out_shape=(
            jax.ShapeDtypeStruct((blocks, rows, cols), jnp.bfloat16),
            jax.ShapeDtypeStruct(w_keyval.shape, jnp.bfloat16),
        )
        + (table,) * 4,
        in_specs=[HBM] * 4,
        out_specs=(VMEM,) * 6,
        scratch_shapes=[
            pltpu.VMEM((rows, d_model), jnp.bfloat16),
            pltpu.VMEM((1, d_model), jnp.float32),
            pltpu.SMEM((rows,), jnp.int32),
            pltpu.SemaphoreType.DMA((4,)),
        ],
        compiler_params=pltpu.CompilerParams(vmem_limit_bytes=8 * 2**20),
    )(in_hbm(hidden_in), in_hbm(norm_gain[None]), in_hbm(w_keyval), in_hbm(lengths))
    spread = exchange(normed, NEAR_GROUPS).reshape(blocks * rows, cols)
    first = jnp.dot(spread, w_query, preferred_element_type=jnp.float32)
    second = jnp.dot(spread, w_keyval, preferred_element_type=jnp.float32)
    partial = jnp.concatenate([first, second], axis=1) * SCALE
    parts = lax.all_to_all(
        partial.astype(jnp.float16).reshape(blocks, rows, cols + hd), "dp", 0, 0, tiled=True
    ).astype(jnp.float32)
    own = pl.pallas_call(
        rotate_kernel,
        out_shape=jax.ShapeDtypeStruct((rows, 16, hd), jnp.bfloat16),
        in_specs=[VMEM] * 5,
        out_specs=VMEM,
        scratch_shapes=[pltpu.VMEM((rows, 16, hd), jnp.float32)],
        compiler_params=pltpu.CompilerParams(vmem_limit_bytes=8 * 2**20),
    )(jnp.sum(parts, axis=0) * (1.0 / SCALE), *tables)
    other = core_swap(own)
    shape = jax.ShapeDtypeStruct((heads, rows, 3 * hd), jnp.float32)
    keep, send = pl.pallas_call(
        attention_kernel,
        out_shape=(shape, shape),
        in_specs=[SMEM, SMEM, VMEM, VMEM, VMEM, HBM],
        out_specs=(VMEM, VMEM),
        scratch_shapes=[
            pltpu.VMEM((rows, half, hd), jnp.bfloat16),
            pltpu.VMEM((rows, 2 * heads, half), jnp.bfloat16),
            pltpu.SemaphoreType.DMA((rows,)),
        ],
        compiler_params=pltpu.CompilerParams(vmem_limit_bytes=24 * 2**20),
    )(parent, lengths, own, other, key_cache, in_hbm(value_cache))
    received = core_swap(send)
    copies = pl.pallas_call(
        merge_kernel,
        out_shape=jax.ShapeDtypeStruct((blocks, rows, cols), jnp.bfloat16),
        in_specs=[VMEM, VMEM],
        out_specs=VMEM,
        compiler_params=pltpu.CompilerParams(vmem_limit_bytes=8 * 2**20),
    )(keep, received)
    spread_heads = lax.all_to_all(copies, "dp", 0, 0, tiled=True)
    partial = jnp.dot(
        spread_heads.reshape(blocks * rows, cols), w_out, preferred_element_type=jnp.float32
    ).astype(jnp.bfloat16)
    gathered = exchange(partial.reshape(blocks, rows, cols), SUM_GROUPS)
    block = jnp.sum(gathered.astype(jnp.float32), axis=0).astype(jnp.bfloat16)
    block = lax.ppermute(block, ("dp", "tensor"), MOVES)
    block = lax.optimization_barrier(jnp.broadcast_to(block[None], (blocks, rows, cols)))
    whole = exchange(block, WHOLE_GROUPS)
    return jnp.transpose(whole, (1, 0, 2)).reshape(rows, d_model)


def solution(mesh):
    return jax.shard_map(
        per_device,
        mesh=mesh,
        in_specs=(
            P("dp", None),
            P(),
            P("dp", "tensor"),
            P("dp", "tensor"),
            P("tensor", "dp"),
            P("dp", "tensor", None, None),
            P("dp", "tensor", None, None),
            P("dp"),
            P("dp"),
        ),
        out_specs=P("dp", None),
        check_vma=False,
    )
```

```python
import jax
import jax.numpy as jnp
import numpy as np
from jax import lax
from jax.experimental import pallas as pl
from jax.experimental.pallas import tpu as pltpu
from jax.sharding import PartitionSpec as P

EPS = 1e-05
SCALE = 128.0
INVERSE = (500000.0 ** (-np.arange(64) * 2.0 / 128)).astype(np.float32)
VMEM = pl.BlockSpec(memory_space=pltpu.VMEM)
SMEM = pl.BlockSpec(memory_space=pltpu.SMEM)
HBM = pl.BlockSpec(memory_space=pltpu.HBM)


def index(x, z_hi, y, z_lo, core):
    return (x * 4 + z_hi) * 16 + y * 4 + z_lo * 2 + core


NEAR_GROUPS = [
    [index(x, z_hi, y, z_lo ^ (z_hi >> 1), core) for x in range(4) for z_hi in range(4)]
    for y in range(4)
    for z_lo in range(2)
    for core in range(2)
]


def holder(j, t):
    return t ^ 2 if t % 4 in (0, 2) else t


SUM_GROUPS = [[j * 16 + (j ^ p) for p in range(16)] for j in range(16)]
MOVES = [
    (j * 16 + t, (j ^ t) * 16 + holder(j, t)) for j in range(16) for t in range(16)
]
WHOLE_GROUPS = [[i * 16 + holder(p, i ^ p) for p in range(16)] for i in range(16)]


def exchange(value, groups):
    return lax.all_to_all(
        value, ("dp", "tensor"), 0, 0, tiled=True, axis_index_groups=groups
    )


def in_hbm(value):
    return pltpu.with_memory_space_constraint(value, pltpu.HBM)


def core_swap(value):
    return lax.ppermute(value, "tensor", [(t, t ^ 1) for t in range(16)])


def norm_kernel(
    hidden_hbm, gain_hbm, weight_hbm, lengths_hbm,
    out, weight, cosine_out, sine_out, kv_cosine_out, kv_sine_out,
    hidden, gain, lengths, sems,
):
    copies = [
        pltpu.make_async_copy(lengths_hbm, lengths, sems.at[0]),
        pltpu.make_async_copy(hidden_hbm, hidden, sems.at[1]),
        pltpu.make_async_copy(gain_hbm, gain, sems.at[2]),
        pltpu.make_async_copy(weight_hbm, weight, sems.at[3]),
    ]
    for copy in copies:
        copy.start()
    rows, hd = cosine_out.shape
    column = lax.broadcasted_iota(jnp.int32, (rows, hd), 1)
    row = lax.broadcasted_iota(jnp.int32, (rows, hd), 0)
    inv = jnp.zeros((rows, hd), jnp.float32)
    for k in range(hd // 2):
        inv = jnp.where(column % (hd // 2) == k, float(INVERSE[k]), inv)
    copies[0].wait()
    position = jnp.zeros((rows, hd), jnp.float32)
    for r in range(rows):
        position = jnp.where(row == r, lengths[r].astype(jnp.float32), position)
    angle = position * inv
    cosine = jnp.cos(angle)
    sine = jnp.where(column < hd // 2, -jnp.sin(angle), jnp.sin(angle))
    is_key = lax.axis_index("tensor") % 2 == 0
    cosine_out[...] = cosine
    sine_out[...] = sine
    kv_cosine_out[...] = jnp.where(is_key, cosine, 1.0)
    kv_sine_out[...] = jnp.where(is_key, sine, 0.0)
    copies[1].wait()
    xf = hidden[...].astype(jnp.float32)
    meansq = jnp.mean(xf * xf, axis=-1, keepdims=True)
    factor = lax.rsqrt(meansq + EPS)
    copies[2].wait()
    blocks, _, width = out.shape
    for k in range(blocks):
        part = slice(k * width, (k + 1) * width)
        out[k] = (xf[:, part] * factor * gain[:, part]).astype(jnp.bfloat16)
    copies[3].wait()


def rotate_kernel(total, cosine, sine, kv_cosine, kv_sine, values, out, turned):
    heads = total.shape[1] // 128 - 1
    for h in range(heads + 1):
        t = total[:, h * 128 : (h + 1) * 128]
        swapped = pltpu.roll(t, 64, 1)
        if h < heads:
            turned[:, h, :] = t * cosine[...] + swapped * sine[...]
        else:
            turned[:, h, :] = t * kv_cosine[...] + swapped * kv_sine[...]
    for r in range(8):
        out[r] = turned[r].astype(jnp.bfloat16)


def attention_kernel(
    parent, lengths, own, other, keys, values, keep, send, weights
):
    rows, _, half, hd = keys.shape
    base = lax.axis_index("dp") * rows
    parity = lax.axis_index("tensor") % 2
    scale = hd ** (-0.5)
    second = parity == 1
    column = lax.broadcasted_iota(jnp.int32, (16, half), 1)
    found = []
    for r in range(rows):
        mine = own[r].astype(jnp.float32)
        theirs = other[r].astype(jnp.float32)
        queries = jnp.concatenate([mine[:8], theirs[:8]], axis=0)
        new_key = jnp.where(second, theirs[8:9], mine[8:9])
        new_value = jnp.where(second, mine[8:9], theirs[8:9])
        newscore = jnp.sum(queries * new_key, axis=-1, keepdims=True) * scale
        newscore = jnp.where(second, newscore, -jnp.inf)
        scores = lax.dot_general(
            queries.astype(jnp.bfloat16),
            keys[parent[r] - base, 0],
            (((1,), (1,)), ((), ())),
            preferred_element_type=jnp.float32,
        )
        limit = lengths[r] - parity * half
        scores = jnp.where(column < limit, scores * scale, -jnp.inf)
        top = jnp.maximum(jnp.max(scores, axis=-1, keepdims=True), newscore)
        weight = jnp.exp(scores - top)
        newweight = jnp.exp(newscore - top)
        total = jnp.sum(weight, axis=-1, keepdims=True) + newweight
        weights[r] = weight.astype(jnp.bfloat16)
        added = newweight.astype(jnp.bfloat16).astype(jnp.float32) * new_value
        found.append((added, top, total))
    for r in range(rows):
        added, top, total = found[r]
        acc = jnp.dot(weights[r], values[parent[r] - base, 0], preferred_element_type=jnp.float32) + added
        top = jnp.broadcast_to(top, acc.shape)
        total = jnp.broadcast_to(total, acc.shape)
        for k, part in enumerate((acc, top, total)):
            keep[:, r, k * hd : (k + 1) * hd] = part[:8]
            send[:, r, k * hd : (k + 1) * hd] = part[8:]


def merge_kernel(mine, theirs, out):
    hd = mine.shape[2] // 3
    for h in range(mine.shape[0]):
        a, b = mine[h], theirs[h]
        highest = jnp.maximum(a[:, hd : 2 * hd], b[:, hd : 2 * hd])
        fa = jnp.exp(a[:, hd : 2 * hd] - highest)
        fb = jnp.exp(b[:, hd : 2 * hd] - highest)
        total = a[:, 2 * hd :] * fa + b[:, 2 * hd :] * fb
        head = ((a[:, :hd] * fa + b[:, :hd] * fb) / total).astype(jnp.bfloat16)
        for k in range(out.shape[0]):
            out[k, :, h * hd : (h + 1) * hd] = head


def per_device(
    hidden_in, norm_gain, w_query, w_keyval, w_out, key_cache, value_cache, parent, lengths
):
    rows, d_model = hidden_in.shape
    hd = key_cache.shape[3]
    half = key_cache.shape[2]
    cols = w_query.shape[1]
    blocks = d_model // cols
    heads = cols // hd
    table = jax.ShapeDtypeStruct((rows, hd), jnp.float32)
    normed, w_keyval, *tables = pl.pallas_call(
        norm_kernel,
        out_shape=(
            jax.ShapeDtypeStruct((blocks, rows, cols), jnp.bfloat16),
            jax.ShapeDtypeStruct(w_keyval.shape, jnp.bfloat16),
        )
        + (table,) * 4,
        in_specs=[HBM] * 4,
        out_specs=(VMEM,) * 6,
        scratch_shapes=[
            pltpu.VMEM((rows, d_model), jnp.bfloat16),
            pltpu.VMEM((1, d_model), jnp.float32),
            pltpu.SMEM((rows,), jnp.int32),
            pltpu.SemaphoreType.DMA((4,)),
        ],
        compiler_params=pltpu.CompilerParams(vmem_limit_bytes=8 * 2**20),
    )(in_hbm(hidden_in), in_hbm(norm_gain[None]), in_hbm(w_keyval), in_hbm(lengths))
    spread = exchange(normed, NEAR_GROUPS).reshape(blocks * rows, cols)
    first = jnp.dot(spread, w_query, preferred_element_type=jnp.float32)
    second = jnp.dot(spread, w_keyval, preferred_element_type=jnp.float32)
    partial = jnp.concatenate([first, second], axis=1) * SCALE
    parts = lax.all_to_all(
        partial.astype(jnp.float16).reshape(blocks, rows, cols + hd), "dp", 0, 0, tiled=True
    ).astype(jnp.float32)
    own = pl.pallas_call(
        rotate_kernel,
        out_shape=jax.ShapeDtypeStruct((rows, 16, hd), jnp.bfloat16),
        in_specs=[VMEM] * 6,
        out_specs=VMEM,
        scratch_shapes=[pltpu.VMEM((rows, 16, hd), jnp.float32)],
        compiler_params=pltpu.CompilerParams(vmem_limit_bytes=8 * 2**20),
            )(jnp.sum(parts, axis=0) * (1.0 / SCALE), *tables, value_cache)
    other = core_swap(own)
    shape = jax.ShapeDtypeStruct((heads, rows, 3 * hd), jnp.float32)
    keep, send = pl.pallas_call(
        attention_kernel,
        out_shape=(shape, shape),
        in_specs=[SMEM, SMEM, VMEM, VMEM, VMEM, VMEM],
        out_specs=(VMEM, VMEM),
        scratch_shapes=[
            pltpu.VMEM((rows, 2 * heads, half), jnp.bfloat16),
        ],
        compiler_params=pltpu.CompilerParams(vmem_limit_bytes=24 * 2**20),
    )(parent, lengths, own, other, key_cache, value_cache)
    received = core_swap(send)
    copies = pl.pallas_call(
        merge_kernel,
        out_shape=jax.ShapeDtypeStruct((blocks, rows, cols), jnp.bfloat16),
        in_specs=[VMEM, VMEM],
        out_specs=VMEM,
        compiler_params=pltpu.CompilerParams(vmem_limit_bytes=8 * 2**20),
    )(keep, received)
    spread_heads = lax.all_to_all(copies, "dp", 0, 0, tiled=True)
    partial = jnp.dot(
        spread_heads.reshape(blocks * rows, cols), w_out, preferred_element_type=jnp.float32
    ).astype(jnp.bfloat16)
    gathered = exchange(partial.reshape(blocks, rows, cols), SUM_GROUPS)
    block = jnp.sum(gathered.astype(jnp.float32), axis=0).astype(jnp.bfloat16)
    block = lax.ppermute(block, ("dp", "tensor"), MOVES)
    block = lax.optimization_barrier(jnp.broadcast_to(block[None], (blocks, rows, cols)))
    whole = exchange(block, WHOLE_GROUPS)
    return jnp.transpose(whole, (1, 0, 2)).reshape(rows, d_model)


def solution(mesh):
    return jax.shard_map(
        per_device,
        mesh=mesh,
        in_specs=(
            P("dp", None),
            P(),
            P("dp", "tensor"),
            P("dp", "tensor"),
            P("tensor", "dp"),
            P("dp", "tensor", None, None),
            P("dp", "tensor", None, None),
            P("dp"),
            P("dp"),
        ),
        out_specs=P("dp", None),
        check_vma=False,
    )
```

```python
import jax
import jax.numpy as jnp
import numpy as np
from jax import lax
from jax.experimental import pallas as pl
from jax.experimental.pallas import tpu as pltpu
from jax.sharding import PartitionSpec as P

EPS = 1e-05
SCALE = 128.0
INVERSE = (500000.0 ** (-np.arange(64) * 2.0 / 128)).astype(np.float32)
VMEM = pl.BlockSpec(memory_space=pltpu.VMEM)
SMEM = pl.BlockSpec(memory_space=pltpu.SMEM)
HBM = pl.BlockSpec(memory_space=pltpu.HBM)


def index(x, z_hi, y, z_lo, core):
    return (x * 4 + z_hi) * 16 + y * 4 + z_lo * 2 + core


NEAR_GROUPS = [
    [index(x, z_hi, y, z_lo ^ (z_hi >> 1), core) for x in range(4) for z_hi in range(4)]
    for y in range(4)
    for z_lo in range(2)
    for core in range(2)
]


X_MOVES = (2, 1, 0, 3)
Z_MOVES = {(1, 0): (1, 0), (0, 0): (3, 1), (0, 1): (2, 1), (1, 1): (0, 0)}


def target(j, t):
    y, z_lo, core = t // 4, t // 2 % 2, t % 2
    z_move, z_lo = Z_MOVES[z_lo, core]
    x, z_hi = (j // 4 + X_MOVES[y]) % 4, (j % 4 + z_move) % 4
    return x * 4 + z_hi, y * 4 + z_lo * 2 + core


SUMMER = {(j, target(j, t)[0]): t for j in range(16) for t in range(16)}
SUM_GROUPS = [[j * 16 + SUMMER[j, p] for p in range(16)] for j in range(16)]
MOVES = [
    (j * 16 + t, target(j, t)[0] * 16 + target(j, t)[1]) for j in range(16) for t in range(16)
]
WHOLE_GROUPS = [[i * 16 + target(p, SUMMER[p, i])[1] for p in range(16)] for i in range(16)]


def exchange(value, groups):
    return lax.all_to_all(
        value, ("dp", "tensor"), 0, 0, tiled=True, axis_index_groups=groups
    )


def in_hbm(value):
    return pltpu.with_memory_space_constraint(value, pltpu.HBM)


def core_swap(value):
    return lax.ppermute(value, "tensor", [(t, t ^ 1) for t in range(16)])


def norm_kernel(
    hidden_hbm, gain_hbm, weight_hbm, lengths_hbm,
    out, weight, cosine_out, sine_out, kv_cosine_out, kv_sine_out,
    hidden, gain, lengths, sems,
):
    copies = [
        pltpu.make_async_copy(lengths_hbm, lengths, sems.at[0]),
        pltpu.make_async_copy(hidden_hbm, hidden, sems.at[1]),
        pltpu.make_async_copy(gain_hbm, gain, sems.at[2]),
        pltpu.make_async_copy(weight_hbm, weight, sems.at[3]),
    ]
    for copy in copies:
        copy.start()
    rows, hd = cosine_out.shape
    column = lax.broadcasted_iota(jnp.int32, (rows, hd), 1)
    row = lax.broadcasted_iota(jnp.int32, (rows, hd), 0)
    inv = jnp.zeros((rows, hd), jnp.float32)
    for k in range(hd // 2):
        inv = jnp.where(column % (hd // 2) == k, float(INVERSE[k]), inv)
    copies[0].wait()
    position = jnp.zeros((rows, hd), jnp.float32)
    for r in range(rows):
        position = jnp.where(row == r, lengths[r].astype(jnp.float32), position)
    angle = position * inv
    cosine = jnp.cos(angle)
    sine = jnp.where(column < hd // 2, -jnp.sin(angle), jnp.sin(angle))
    is_key = lax.axis_index("tensor") % 2 == 0
    cosine_out[...] = cosine
    sine_out[...] = sine
    kv_cosine_out[...] = jnp.where(is_key, cosine, 1.0)
    kv_sine_out[...] = jnp.where(is_key, sine, 0.0)
    copies[1].wait()
    xf = hidden[...].astype(jnp.float32)
    meansq = jnp.mean(xf * xf, axis=-1, keepdims=True)
    factor = lax.rsqrt(meansq + EPS)
    copies[2].wait()
    blocks, _, width = out.shape
    for k in range(blocks):
        part = slice(k * width, (k + 1) * width)
        out[k] = (xf[:, part] * factor * gain[:, part]).astype(jnp.bfloat16)
    copies[3].wait()


def rotate_kernel(total, cosine, sine, kv_cosine, kv_sine, values, out, turned):
    heads = total.shape[1] // 128 - 1
    for h in range(heads + 1):
        t = total[:, h * 128 : (h + 1) * 128]
        swapped = pltpu.roll(t, 64, 1)
        if h < heads:
            turned[:, h, :] = t * cosine[...] + swapped * sine[...]
        else:
            turned[:, h, :] = t * kv_cosine[...] + swapped * kv_sine[...]
    for r in range(8):
        out[r] = turned[r].astype(jnp.bfloat16)


def attention_kernel(
    parent, lengths, own, other, keys, values, keep, send, weights
):
    rows, _, half, hd = keys.shape
    base = lax.axis_index("dp") * rows
    parity = lax.axis_index("tensor") % 2
    scale = hd ** (-0.5)
    second = parity == 1
    column = lax.broadcasted_iota(jnp.int32, (16, half), 1)
    found = []
    for r in range(rows):
        mine = own[r].astype(jnp.float32)
        theirs = other[r].astype(jnp.float32)
        queries = jnp.concatenate([mine[:8], theirs[:8]], axis=0)
        new_key = jnp.where(second, theirs[8:9], mine[8:9])
        new_value = jnp.where(second, mine[8:9], theirs[8:9])
        newscore = jnp.sum(queries * new_key, axis=-1, keepdims=True) * scale
        newscore = jnp.where(second, newscore, -jnp.inf)
        scores = lax.dot_general(
            queries.astype(jnp.bfloat16),
            keys[parent[r] - base, 0],
            (((1,), (1,)), ((), ())),
            preferred_element_type=jnp.float32,
        )
        limit = lengths[r] - parity * half
        scores = jnp.where(column < limit, scores * scale, -jnp.inf)
        top = jnp.maximum(jnp.max(scores, axis=-1, keepdims=True), newscore)
        weight = jnp.exp(scores - top)
        newweight = jnp.exp(newscore - top)
        total = jnp.sum(weight, axis=-1, keepdims=True) + newweight
        weights[r] = weight.astype(jnp.bfloat16)
        added = newweight.astype(jnp.bfloat16).astype(jnp.float32) * new_value
        found.append((added, top, total))
    for r in range(rows):
        added, top, total = found[r]
        acc = jnp.dot(weights[r], values[parent[r] - base, 0], preferred_element_type=jnp.float32) + added
        top = jnp.broadcast_to(top, acc.shape)
        total = jnp.broadcast_to(total, acc.shape)
        for k, part in enumerate((acc, top, total)):
            keep[:, r, k * hd : (k + 1) * hd] = part[:8]
            send[:, r, k * hd : (k + 1) * hd] = part[8:]


def merge_kernel(mine, theirs, out):
    hd = mine.shape[2] // 3
    for h in range(mine.shape[0]):
        a, b = mine[h], theirs[h]
        highest = jnp.maximum(a[:, hd : 2 * hd], b[:, hd : 2 * hd])
        fa = jnp.exp(a[:, hd : 2 * hd] - highest)
        fb = jnp.exp(b[:, hd : 2 * hd] - highest)
        total = a[:, 2 * hd :] * fa + b[:, 2 * hd :] * fb
        head = ((a[:, :hd] * fa + b[:, :hd] * fb) / total).astype(jnp.bfloat16)
        for k in range(out.shape[0]):
            out[k, :, h * hd : (h + 1) * hd] = head


def per_device(
    hidden_in, norm_gain, w_query, w_keyval, w_out, key_cache, value_cache, parent, lengths
):
    rows, d_model = hidden_in.shape
    hd = key_cache.shape[3]
    half = key_cache.shape[2]
    cols = w_query.shape[1]
    blocks = d_model // cols
    heads = cols // hd
    table = jax.ShapeDtypeStruct((rows, hd), jnp.float32)
    normed, w_keyval, *tables = pl.pallas_call(
        norm_kernel,
        out_shape=(
            jax.ShapeDtypeStruct((blocks, rows, cols), jnp.bfloat16),
            jax.ShapeDtypeStruct(w_keyval.shape, jnp.bfloat16),
        )
        + (table,) * 4,
        in_specs=[HBM] * 4,
        out_specs=(VMEM,) * 6,
        scratch_shapes=[
            pltpu.VMEM((rows, d_model), jnp.bfloat16),
            pltpu.VMEM((1, d_model), jnp.float32),
            pltpu.SMEM((rows,), jnp.int32),
            pltpu.SemaphoreType.DMA((4,)),
        ],
        compiler_params=pltpu.CompilerParams(vmem_limit_bytes=8 * 2**20),
    )(in_hbm(hidden_in), in_hbm(norm_gain[None]), in_hbm(w_keyval), in_hbm(lengths))
    spread = exchange(normed, NEAR_GROUPS).reshape(blocks * rows, cols)
    first = jnp.dot(spread, w_query, preferred_element_type=jnp.float32)
    second = jnp.dot(spread, w_keyval, preferred_element_type=jnp.float32)
    partial = jnp.concatenate([first, second], axis=1) * SCALE
    parts = lax.all_to_all(
        partial.astype(jnp.float16).reshape(blocks, rows, cols + hd), "dp", 0, 0, tiled=True
    ).astype(jnp.float32)
    own = pl.pallas_call(
        rotate_kernel,
        out_shape=jax.ShapeDtypeStruct((rows, 16, hd), jnp.bfloat16),
        in_specs=[VMEM] * 6,
        out_specs=VMEM,
        scratch_shapes=[pltpu.VMEM((rows, 16, hd), jnp.float32)],
        compiler_params=pltpu.CompilerParams(vmem_limit_bytes=8 * 2**20),
            )(jnp.sum(parts, axis=0) * (1.0 / SCALE), *tables, value_cache)
    other = core_swap(own)
    shape = jax.ShapeDtypeStruct((heads, rows, 3 * hd), jnp.float32)
    keep, send = pl.pallas_call(
        attention_kernel,
        out_shape=(shape, shape),
        in_specs=[SMEM, SMEM, VMEM, VMEM, VMEM, VMEM],
        out_specs=(VMEM, VMEM),
        scratch_shapes=[
            pltpu.VMEM((rows, 2 * heads, half), jnp.bfloat16),
        ],
        compiler_params=pltpu.CompilerParams(vmem_limit_bytes=24 * 2**20),
    )(parent, lengths, own, other, key_cache, value_cache)
    received = core_swap(send)
    copies = pl.pallas_call(
        merge_kernel,
        out_shape=jax.ShapeDtypeStruct((blocks, rows, cols), jnp.bfloat16),
        in_specs=[VMEM, VMEM],
        out_specs=VMEM,
        compiler_params=pltpu.CompilerParams(vmem_limit_bytes=8 * 2**20),
    )(keep, received)
    spread_heads = lax.all_to_all(copies, "dp", 0, 0, tiled=True)
    partial = jnp.dot(
        spread_heads.reshape(blocks * rows, cols), w_out, preferred_element_type=jnp.float32
    ).astype(jnp.bfloat16)
    gathered = exchange(partial.reshape(blocks, rows, cols), SUM_GROUPS)
    block = jnp.sum(gathered.astype(jnp.float32), axis=0).astype(jnp.bfloat16)
    block = lax.ppermute(block, ("dp", "tensor"), MOVES)
    block = lax.optimization_barrier(jnp.broadcast_to(block[None], (blocks, rows, cols)))
    whole = exchange(block, WHOLE_GROUPS)
    return jnp.transpose(whole, (1, 0, 2)).reshape(rows, d_model)


def solution(mesh):
    return jax.shard_map(
        per_device,
        mesh=mesh,
        in_specs=(
            P("dp", None),
            P(),
            P("dp", "tensor"),
            P("dp", "tensor"),
            P("tensor", "dp"),
            P("dp", "tensor", None, None),
            P("dp", "tensor", None, None),
            P("dp"),
            P("dp"),
        ),
        out_specs=P("dp", None),
        check_vma=False,
    )
```

```python
import jax
import jax.numpy as jnp
import numpy as np
from jax import lax
from jax.experimental import pallas as pl
from jax.experimental.pallas import tpu as pltpu
from jax.sharding import PartitionSpec as P

EPS = 1e-05
SCALE = 128.0
INVERSE = (500000.0 ** (-np.arange(64) * 2.0 / 128)).astype(np.float32)
VMEM = pl.BlockSpec(memory_space=pltpu.VMEM)
SMEM = pl.BlockSpec(memory_space=pltpu.SMEM)
HBM = pl.BlockSpec(memory_space=pltpu.HBM)


def index(x, z_hi, y, z_lo, core):
    return (x * 4 + z_hi) * 16 + y * 4 + z_lo * 2 + core


NEAR_GROUPS = [
    [index(x, z_hi, y, z_lo ^ (z_hi >> 1), core) for x in range(4) for z_hi in range(4)]
    for y in range(4)
    for z_lo in range(2)
    for core in range(2)
]


X_MOVES = (2, 1, 0, 3)
Z_MOVES = {(1, 0): (1, 0), (0, 0): (3, 1), (0, 1): (2, 1), (1, 1): (0, 0)}


def target(j, t):
    y, z_lo, core = t // 4, t // 2 % 2, t % 2
    z_move, z_lo = Z_MOVES[z_lo, core]
    x_move = X_MOVES[y] + (2 if z_move == 2 else 0)
    x, z_hi = (j // 4 + x_move) % 4, (j % 4 + z_move) % 4
    return x * 4 + z_hi, y * 4 + z_lo * 2 + core


SUMMER = {(j, target(j, t)[0]): t for j in range(16) for t in range(16)}
SUM_GROUPS = [[j * 16 + SUMMER[j, p] for p in range(16)] for j in range(16)]
MOVES = [
    (j * 16 + t, target(j, t)[0] * 16 + target(j, t)[1]) for j in range(16) for t in range(16)
]
WHOLE_GROUPS = [[i * 16 + target(p, SUMMER[p, i])[1] for p in range(16)] for i in range(16)]


def exchange(value, groups):
    return lax.all_to_all(
        value, ("dp", "tensor"), 0, 0, tiled=True, axis_index_groups=groups
    )


def in_hbm(value):
    return pltpu.with_memory_space_constraint(value, pltpu.HBM)


def core_swap(value):
    return lax.ppermute(value, "tensor", [(t, t ^ 1) for t in range(16)])


def norm_kernel(
    hidden_hbm, gain_hbm, weight_hbm, lengths_hbm,
    out, weight, cosine_out, sine_out, kv_cosine_out, kv_sine_out,
    hidden, gain, lengths, sems,
):
    copies = [
        pltpu.make_async_copy(lengths_hbm, lengths, sems.at[0]),
        pltpu.make_async_copy(hidden_hbm, hidden, sems.at[1]),
        pltpu.make_async_copy(gain_hbm, gain, sems.at[2]),
        pltpu.make_async_copy(weight_hbm, weight, sems.at[3]),
    ]
    for copy in copies:
        copy.start()
    rows, hd = cosine_out.shape
    column = lax.broadcasted_iota(jnp.int32, (rows, hd), 1)
    row = lax.broadcasted_iota(jnp.int32, (rows, hd), 0)
    inv = jnp.zeros((rows, hd), jnp.float32)
    for k in range(hd // 2):
        inv = jnp.where(column % (hd // 2) == k, float(INVERSE[k]), inv)
    copies[0].wait()
    position = jnp.zeros((rows, hd), jnp.float32)
    for r in range(rows):
        position = jnp.where(row == r, lengths[r].astype(jnp.float32), position)
    angle = position * inv
    cosine = jnp.cos(angle)
    sine = jnp.where(column < hd // 2, -jnp.sin(angle), jnp.sin(angle))
    is_key = lax.axis_index("tensor") % 2 == 0
    cosine_out[...] = cosine
    sine_out[...] = sine
    kv_cosine_out[...] = jnp.where(is_key, cosine, 1.0)
    kv_sine_out[...] = jnp.where(is_key, sine, 0.0)
    copies[1].wait()
    xf = hidden[...].astype(jnp.float32)
    meansq = jnp.mean(xf * xf, axis=-1, keepdims=True)
    factor = lax.rsqrt(meansq + EPS)
    copies[2].wait()
    blocks, _, width = out.shape
    for k in range(blocks):
        part = slice(k * width, (k + 1) * width)
        out[k] = (xf[:, part] * factor * gain[:, part]).astype(jnp.bfloat16)
    copies[3].wait()


def rotate_kernel(total, cosine, sine, kv_cosine, kv_sine, values, out, turned):
    heads = total.shape[1] // 128 - 1
    for h in range(heads + 1):
        t = total[:, h * 128 : (h + 1) * 128]
        swapped = pltpu.roll(t, 64, 1)
        if h < heads:
            turned[:, h, :] = t * cosine[...] + swapped * sine[...]
        else:
            turned[:, h, :] = t * kv_cosine[...] + swapped * kv_sine[...]
    for r in range(8):
        out[r] = turned[r].astype(jnp.bfloat16)


def attention_kernel(
    parent, lengths, own, other, keys, values, keep, send, weights
):
    rows, _, half, hd = keys.shape
    base = lax.axis_index("dp") * rows
    parity = lax.axis_index("tensor") % 2
    scale = hd ** (-0.5)
    second = parity == 1
    column = lax.broadcasted_iota(jnp.int32, (16, half), 1)
    found = []
    for r in range(rows):
        mine = own[r].astype(jnp.float32)
        theirs = other[r].astype(jnp.float32)
        queries = jnp.concatenate([mine[:8], theirs[:8]], axis=0)
        new_key = jnp.where(second, theirs[8:9], mine[8:9])
        new_value = jnp.where(second, mine[8:9], theirs[8:9])
        newscore = jnp.sum(queries * new_key, axis=-1, keepdims=True) * scale
        newscore = jnp.where(second, newscore, -jnp.inf)
        scores = lax.dot_general(
            queries.astype(jnp.bfloat16),
            keys[parent[r] - base, 0],
            (((1,), (1,)), ((), ())),
            preferred_element_type=jnp.float32,
        )
        limit = lengths[r] - parity * half
        scores = jnp.where(column < limit, scores * scale, -jnp.inf)
        top = jnp.maximum(jnp.max(scores, axis=-1, keepdims=True), newscore)
        weight = jnp.exp(scores - top)
        newweight = jnp.exp(newscore - top)
        total = jnp.sum(weight, axis=-1, keepdims=True) + newweight
        weights[r] = weight.astype(jnp.bfloat16)
        added = newweight.astype(jnp.bfloat16).astype(jnp.float32) * new_value
        found.append((added, top, total))
    for r in range(rows):
        added, top, total = found[r]
        acc = jnp.dot(weights[r], values[parent[r] - base, 0], preferred_element_type=jnp.float32) + added
        top = jnp.broadcast_to(top, acc.shape)
        total = jnp.broadcast_to(total, acc.shape)
        for k, part in enumerate((acc, top, total)):
            keep[:, r, k * hd : (k + 1) * hd] = part[:8]
            send[:, r, k * hd : (k + 1) * hd] = part[8:]


def merge_kernel(mine, theirs, out):
    hd = mine.shape[2] // 3
    for h in range(mine.shape[0]):
        a, b = mine[h], theirs[h]
        highest = jnp.maximum(a[:, hd : 2 * hd], b[:, hd : 2 * hd])
        fa = jnp.exp(a[:, hd : 2 * hd] - highest)
        fb = jnp.exp(b[:, hd : 2 * hd] - highest)
        total = a[:, 2 * hd :] * fa + b[:, 2 * hd :] * fb
        head = ((a[:, :hd] * fa + b[:, :hd] * fb) / total).astype(jnp.bfloat16)
        for k in range(out.shape[0]):
            out[k, :, h * hd : (h + 1) * hd] = head


def per_device(
    hidden_in, norm_gain, w_query, w_keyval, w_out, key_cache, value_cache, parent, lengths
):
    rows, d_model = hidden_in.shape
    hd = key_cache.shape[3]
    half = key_cache.shape[2]
    cols = w_query.shape[1]
    blocks = d_model // cols
    heads = cols // hd
    table = jax.ShapeDtypeStruct((rows, hd), jnp.float32)
    normed, w_keyval, *tables = pl.pallas_call(
        norm_kernel,
        out_shape=(
            jax.ShapeDtypeStruct((blocks, rows, cols), jnp.bfloat16),
            jax.ShapeDtypeStruct(w_keyval.shape, jnp.bfloat16),
        )
        + (table,) * 4,
        in_specs=[HBM] * 4,
        out_specs=(VMEM,) * 6,
        scratch_shapes=[
            pltpu.VMEM((rows, d_model), jnp.bfloat16),
            pltpu.VMEM((1, d_model), jnp.float32),
            pltpu.SMEM((rows,), jnp.int32),
            pltpu.SemaphoreType.DMA((4,)),
        ],
        compiler_params=pltpu.CompilerParams(vmem_limit_bytes=8 * 2**20),
    )(in_hbm(hidden_in), in_hbm(norm_gain[None]), in_hbm(w_keyval), in_hbm(lengths))
    spread = exchange(normed, NEAR_GROUPS).reshape(blocks * rows, cols)
    first = jnp.dot(spread, w_query, preferred_element_type=jnp.float32)
    second = jnp.dot(spread, w_keyval, preferred_element_type=jnp.float32)
    partial = jnp.concatenate([first, second], axis=1) * SCALE
    parts = lax.all_to_all(
        partial.astype(jnp.float16).reshape(blocks, rows, cols + hd), "dp", 0, 0, tiled=True
    ).astype(jnp.float32)
    own = pl.pallas_call(
        rotate_kernel,
        out_shape=jax.ShapeDtypeStruct((rows, 16, hd), jnp.bfloat16),
        in_specs=[VMEM] * 6,
        out_specs=VMEM,
        scratch_shapes=[pltpu.VMEM((rows, 16, hd), jnp.float32)],
        compiler_params=pltpu.CompilerParams(vmem_limit_bytes=8 * 2**20),
            )(jnp.sum(parts, axis=0) * (1.0 / SCALE), *tables, value_cache)
    other = core_swap(own)
    shape = jax.ShapeDtypeStruct((heads, rows, 3 * hd), jnp.float32)
    keep, send = pl.pallas_call(
        attention_kernel,
        out_shape=(shape, shape),
        in_specs=[SMEM, SMEM, VMEM, VMEM, VMEM, VMEM],
        out_specs=(VMEM, VMEM),
        scratch_shapes=[
            pltpu.VMEM((rows, 2 * heads, half), jnp.bfloat16),
        ],
        compiler_params=pltpu.CompilerParams(vmem_limit_bytes=24 * 2**20),
    )(parent, lengths, own, other, key_cache, value_cache)
    received = core_swap(send)
    copies = pl.pallas_call(
        merge_kernel,
        out_shape=jax.ShapeDtypeStruct((blocks, rows, cols), jnp.bfloat16),
        in_specs=[VMEM, VMEM],
        out_specs=VMEM,
        compiler_params=pltpu.CompilerParams(vmem_limit_bytes=8 * 2**20),
    )(keep, received)
    spread_heads = lax.all_to_all(copies, "dp", 0, 0, tiled=True)
    partial = jnp.dot(
        spread_heads.reshape(blocks * rows, cols), w_out, preferred_element_type=jnp.float32
    ).astype(jnp.bfloat16)
    gathered = exchange(partial.reshape(blocks, rows, cols), SUM_GROUPS)
    block = jnp.sum(gathered.astype(jnp.float32), axis=0).astype(jnp.bfloat16)
    block = lax.ppermute(block, ("dp", "tensor"), MOVES)
    block = lax.optimization_barrier(jnp.broadcast_to(block[None], (blocks, rows, cols)))
    whole = exchange(block, WHOLE_GROUPS)
    return jnp.transpose(whole, (1, 0, 2)).reshape(rows, d_model)


def solution(mesh):
    return jax.shard_map(
        per_device,
        mesh=mesh,
        in_specs=(
            P("dp", None),
            P(),
            P("dp", "tensor"),
            P("dp", "tensor"),
            P("tensor", "dp"),
            P("dp", "tensor", None, None),
            P("dp", "tensor", None, None),
            P("dp"),
            P("dp"),
        ),
        out_specs=P("dp", None),
        check_vma=False,
    )
```

```python
import jax
import jax.numpy as jnp
import numpy as np
from jax import lax
from jax.experimental import pallas as pl
from jax.experimental.pallas import tpu as pltpu
from jax.sharding import PartitionSpec as P

EPS = 1e-05
SCALE = 128.0
INVERSE = (500000.0 ** (-np.arange(64) * 2.0 / 128)).astype(np.float32)
VMEM = pl.BlockSpec(memory_space=pltpu.VMEM)
SMEM = pl.BlockSpec(memory_space=pltpu.SMEM)
HBM = pl.BlockSpec(memory_space=pltpu.HBM)


def index(x, z_hi, y, z_lo, core):
    return (x * 4 + z_hi) * 16 + y * 4 + z_lo * 2 + core


NEAR_GROUPS = [
    [index(x, z_hi, y, z_lo ^ (z_hi >> 1), core) for x in range(4) for z_hi in range(4)]
    for y in range(4)
    for z_lo in range(2)
    for core in range(2)
]


X_MOVES = (2, 1, 0, 3)
Z_MOVES = {(1, 0): (1, 0), (0, 0): (3, 1), (0, 1): (2, 1), (1, 1): (0, 0)}


def target(j, t):
    y, z_lo, core = t // 4, t // 2 % 2, t % 2
    z_move, z_lo = Z_MOVES[z_lo, core]
    x_move = X_MOVES[y] + (2 if z_move == 2 else 0)
    x, z_hi = (j // 4 + x_move) % 4, (j % 4 + z_move) % 4
    return x * 4 + z_hi, y * 4 + z_lo * 2 + core


SUMMER = {(j, target(j, t)[0]): t for j in range(16) for t in range(16)}
SUM_GROUPS = [[j * 16 + SUMMER[j, p] for p in range(16)] for j in range(16)]
MOVES = [
    (j * 16 + t, target(j, t)[0] * 16 + target(j, t)[1]) for j in range(16) for t in range(16)
]
WHOLE_GROUPS = [[i * 16 + target(p, SUMMER[p, i])[1] for p in range(16)] for i in range(16)]


def exchange(value, groups):
    return lax.all_to_all(
        value, ("dp", "tensor"), 0, 0, tiled=True, axis_index_groups=groups
    )


def in_hbm(value):
    return pltpu.with_memory_space_constraint(value, pltpu.HBM)


def core_swap(value):
    return lax.ppermute(value, "tensor", [(t, t ^ 1) for t in range(16)])


def norm_kernel(
    hidden_hbm, gain_hbm, weight_hbm, lengths_hbm,
    out, weight, cosine_out, sine_out, kv_cosine_out, kv_sine_out,
    hidden, gain, lengths, sems,
):
    copies = [
        pltpu.make_async_copy(lengths_hbm, lengths, sems.at[0]),
        pltpu.make_async_copy(hidden_hbm, hidden, sems.at[1]),
        pltpu.make_async_copy(gain_hbm, gain, sems.at[2]),
        pltpu.make_async_copy(weight_hbm, weight, sems.at[3]),
    ]
    for copy in copies:
        copy.start()
    rows, hd = cosine_out.shape
    column = lax.broadcasted_iota(jnp.int32, (rows, hd), 1)
    row = lax.broadcasted_iota(jnp.int32, (rows, hd), 0)
    inv = jnp.zeros((rows, hd), jnp.float32)
    for k in range(hd // 2):
        inv = jnp.where(column % (hd // 2) == k, float(INVERSE[k]), inv)
    copies[0].wait()
    position = jnp.zeros((rows, hd), jnp.float32)
    for r in range(rows):
        position = jnp.where(row == r, lengths[r].astype(jnp.float32), position)
    angle = position * inv
    cosine = jnp.cos(angle)
    sine = jnp.where(column < hd // 2, -jnp.sin(angle), jnp.sin(angle))
    is_key = lax.axis_index("tensor") % 2 == 0
    cosine_out[...] = cosine
    sine_out[...] = sine
    kv_cosine_out[...] = jnp.where(is_key, cosine, 1.0)
    kv_sine_out[...] = jnp.where(is_key, sine, 0.0)
    copies[1].wait()
    xf = hidden[...].astype(jnp.float32)
    meansq = jnp.mean(xf * xf, axis=-1, keepdims=True)
    factor = lax.rsqrt(meansq + EPS)
    copies[2].wait()
    blocks, _, width = out.shape
    for k in range(blocks):
        part = slice(k * width, (k + 1) * width)
        out[k] = (xf[:, part] * factor * gain[:, part]).astype(jnp.bfloat16)
    copies[3].wait()


def rotate_kernel(total, cosine, sine, kv_cosine, kv_sine, values, out, turned):
    heads = total.shape[1] // 128 - 1
    for h in range(heads + 1):
        t = total[:, h * 128 : (h + 1) * 128]
        swapped = pltpu.roll(t, 64, 1)
        if h < heads:
            turned[:, h, :] = t * cosine[...] + swapped * sine[...]
        else:
            turned[:, h, :] = t * kv_cosine[...] + swapped * kv_sine[...]
    for r in range(8):
        out[r] = turned[r].astype(jnp.bfloat16)


def attention_kernel(
    parent, lengths, own, other, keys, values, keep, send, weights
):
    rows, _, half, hd = keys.shape
    base = lax.axis_index("dp") * rows
    parity = lax.axis_index("tensor") % 2
    scale = hd ** (-0.5)
    second = parity == 1
    column = lax.broadcasted_iota(jnp.int32, (16, half), 1)
    found = []
    for r in range(rows):
        mine = own[r].astype(jnp.float32)
        theirs = other[r].astype(jnp.float32)
        queries = jnp.concatenate([mine[:8], theirs[:8]], axis=0)
        new_key = jnp.where(second, theirs[8:9], mine[8:9])
        new_value = jnp.where(second, mine[8:9], theirs[8:9])
        newscore = jnp.sum(queries * new_key, axis=-1, keepdims=True) * scale
        newscore = jnp.where(second, newscore, -jnp.inf)
        scores = lax.dot_general(
            queries.astype(jnp.bfloat16),
            keys[parent[r] - base, 0],
            (((1,), (1,)), ((), ())),
            preferred_element_type=jnp.float32,
        )
        limit = lengths[r] - parity * half
        scores = jnp.where(column < limit, scores * scale, -jnp.inf)
        top = jnp.maximum(jnp.max(scores, axis=-1, keepdims=True), newscore)
        weight = jnp.exp(scores - top)
        newweight = jnp.exp(newscore - top)
        total = jnp.sum(weight, axis=-1, keepdims=True) + newweight
        weights[r] = weight.astype(jnp.bfloat16)
        added = newweight.astype(jnp.bfloat16).astype(jnp.float32) * new_value
        found.append((added, top, total))
    for r in range(rows):
        added, top, total = found[r]
        acc = jnp.dot(weights[r], values[parent[r] - base, 0], preferred_element_type=jnp.float32) + added
        stats = jnp.where(column[:, :hd] < hd // 2, top, total)
        for k, part in enumerate((acc, stats)):
            keep[:, r, k * hd : (k + 1) * hd] = part[:8]
            send[:, r, k * hd : (k + 1) * hd] = part[8:]


def merge_kernel(mine, theirs, out):
    heads, rows, width = mine.shape
    hd = width // 2
    first = lax.broadcasted_iota(jnp.int32, (rows, hd), 1) < hd // 2

    def spread(stats):
        turned = pltpu.roll(stats, hd // 2, 1)
        return jnp.where(first, stats, turned), jnp.where(first, turned, stats)

    for h in range(heads):
        a, b = mine[h], theirs[h]
        top_a, total_a = spread(a[:, hd:])
        top_b, total_b = spread(b[:, hd:])
        highest = jnp.maximum(top_a, top_b)
        fa = jnp.exp(top_a - highest)
        fb = jnp.exp(top_b - highest)
        total = total_a * fa + total_b * fb
        head = ((a[:, :hd] * fa + b[:, :hd] * fb) / total).astype(jnp.bfloat16)
        for k in range(out.shape[0]):
            out[k, :, h * hd : (h + 1) * hd] = head


def per_device(
    hidden_in, norm_gain, w_query, w_keyval, w_out, key_cache, value_cache, parent, lengths
):
    rows, d_model = hidden_in.shape
    hd = key_cache.shape[3]
    half = key_cache.shape[2]
    cols = w_query.shape[1]
    blocks = d_model // cols
    heads = cols // hd
    table = jax.ShapeDtypeStruct((rows, hd), jnp.float32)
    normed, w_keyval, *tables = pl.pallas_call(
        norm_kernel,
        out_shape=(
            jax.ShapeDtypeStruct((blocks, rows, cols), jnp.bfloat16),
            jax.ShapeDtypeStruct(w_keyval.shape, jnp.bfloat16),
        )
        + (table,) * 4,
        in_specs=[HBM] * 4,
        out_specs=(VMEM,) * 6,
        scratch_shapes=[
            pltpu.VMEM((rows, d_model), jnp.bfloat16),
            pltpu.VMEM((1, d_model), jnp.float32),
            pltpu.SMEM((rows,), jnp.int32),
            pltpu.SemaphoreType.DMA((4,)),
        ],
        compiler_params=pltpu.CompilerParams(vmem_limit_bytes=8 * 2**20),
    )(in_hbm(hidden_in), in_hbm(norm_gain[None]), in_hbm(w_keyval), in_hbm(lengths))
    spread = exchange(normed, NEAR_GROUPS).reshape(blocks * rows, cols)
    first = jnp.dot(spread, w_query, preferred_element_type=jnp.float32)
    second = jnp.dot(spread, w_keyval, preferred_element_type=jnp.float32)
    partial = jnp.concatenate([first, second], axis=1) * SCALE
    parts = lax.all_to_all(
        partial.astype(jnp.float16).reshape(blocks, rows, cols + hd), "dp", 0, 0, tiled=True
    ).astype(jnp.float32)
    own = pl.pallas_call(
        rotate_kernel,
        out_shape=jax.ShapeDtypeStruct((rows, 16, hd), jnp.bfloat16),
        in_specs=[VMEM] * 6,
        out_specs=VMEM,
        scratch_shapes=[pltpu.VMEM((rows, 16, hd), jnp.float32)],
        compiler_params=pltpu.CompilerParams(vmem_limit_bytes=8 * 2**20),
            )(jnp.sum(parts, axis=0) * (1.0 / SCALE), *tables, value_cache)
    other = core_swap(own)
    shape = jax.ShapeDtypeStruct((heads, rows, 2 * hd), jnp.float32)
    keep, send = pl.pallas_call(
        attention_kernel,
        out_shape=(shape, shape),
        in_specs=[SMEM, SMEM, VMEM, VMEM, VMEM, VMEM],
        out_specs=(VMEM, VMEM),
        scratch_shapes=[
            pltpu.VMEM((rows, 2 * heads, half), jnp.bfloat16),
        ],
        compiler_params=pltpu.CompilerParams(vmem_limit_bytes=24 * 2**20),
    )(parent, lengths, own, other, key_cache, value_cache)
    received = core_swap(send)
    copies = pl.pallas_call(
        merge_kernel,
        out_shape=jax.ShapeDtypeStruct((blocks, rows, cols), jnp.bfloat16),
        in_specs=[VMEM, VMEM],
        out_specs=VMEM,
        compiler_params=pltpu.CompilerParams(vmem_limit_bytes=8 * 2**20),
    )(keep, received)
    spread_heads = lax.all_to_all(copies, "dp", 0, 0, tiled=True)
    partial = jnp.dot(
        spread_heads.reshape(blocks * rows, cols), w_out, preferred_element_type=jnp.float32
    ).astype(jnp.bfloat16)
    gathered = exchange(partial.reshape(blocks, rows, cols), SUM_GROUPS)
    block = jnp.sum(gathered.astype(jnp.float32), axis=0).astype(jnp.bfloat16)
    block = lax.ppermute(block, ("dp", "tensor"), MOVES)
    block = lax.optimization_barrier(jnp.broadcast_to(block[None], (blocks, rows, cols)))
    whole = exchange(block, WHOLE_GROUPS)
    return jnp.transpose(whole, (1, 0, 2)).reshape(rows, d_model)


def solution(mesh):
    return jax.shard_map(
        per_device,
        mesh=mesh,
        in_specs=(
            P("dp", None),
            P(),
            P("dp", "tensor"),
            P("dp", "tensor"),
            P("tensor", "dp"),
            P("dp", "tensor", None, None),
            P("dp", "tensor", None, None),
            P("dp"),
            P("dp"),
        ),
        out_specs=P("dp", None),
        check_vma=False,
    )
```
